256 devices in a mesh: tm: 16 (over x_lo, y, core), band: 16 (over x_hi, z).
Axes of the slice: x: 4 (x_hi: 2, x_lo: 2; x = x_hi * 2 + x_lo), y: 4, z: 8, core: 2. Of those that a mesh axis runs over, the one named last changes fastest.
Arguments:
- frames: bfloat16 [512, 65536], P('tm', 'band'), may hold values from 0.2 to 5
- cycle_map: int32 [65536], P('band'), may hold values from 0 to 63, as said below
Outputs:
- correlation: float32 [64, 512, 512], P('band', 'tm')
The draws below stay inside these ranges and needn't reach their ends.
Inputs may be any that keep to these rules, and one draw needn't show every extreme that they name: `cycle_map`: within each band of 4096 pixels the cycle indices never fall; in every band each cycle has from 32 to 96 pixels, and some cycle has exactly 96.
All inputs are finite; a program needn't handle non-finite values.
Results may differ from the reference program's by a relative error of at most 0.00048.
Values may be sent and summed in bfloat16 or wider, within the bound.
A program may use at most 128 MiB of HBM per device.

```python
import math
import jax
import jax.numpy as jnp
from jax import lax

CYCLES = 64
PB = 4096
FRAMES = 512
PIXELS = 65536
N_BAND = 16


def draw_frames(key, part):
    key = jax.random.fold_in(key, 11)
    key_band, key_frame, key_pixel = jax.random.split(key, 3)
    band_level = jax.random.uniform(key_band, (N_BAND,), jnp.float32, -0.6, 0.6)
    frame_level = jax.random.uniform(key_frame, (FRAMES, 1), jnp.float32, -0.3, 0.3)
    column_level = jnp.repeat(band_level, PB, total_repeat_length=PIXELS)
    noise = jax.random.uniform(key_pixel, (FRAMES, PIXELS), jnp.float32, math.log(0.3), math.log(3.3))
    logged = column_level[None, :] + frame_level + noise
    logged = jnp.clip(logged, math.log(0.21), math.log(4.9))
    return jnp.exp(logged).astype(jnp.bfloat16)


def draw_cycle_map(key, part):
    key = jax.random.fold_in(key, 7)
    key_one, key_two, key_three = jax.random.split(key, 3)
    base = PB // CYCLES
    pair_count = CYCLES // 2
    first = jax.random.randint(key_one, (N_BAND, pair_count), base // 2, base + base // 2 + 1, dtype=jnp.int32)
    picked = jax.random.randint(key_two, (N_BAND,), 0, pair_count, dtype=jnp.int32)
    first = jnp.where(jnp.arange(pair_count, dtype=jnp.int32)[None, :] == picked[:, None], base + base // 2, first)
    second = 2 * base - first
    paired = jnp.concatenate([first, second], axis=1).astype(jnp.int32)
    scores = jax.random.randint(key_three, (N_BAND, CYCLES), 0, 2 ** 20, dtype=jnp.int32) * CYCLES
    scores = scores + jnp.arange(CYCLES, dtype=jnp.int32)[None, :]
    order = jnp.argsort(scores, axis=1).astype(jnp.int32)
    lengths = jnp.take_along_axis(paired, order, axis=1).astype(jnp.int32)
    ends = jnp.cumsum(lengths, axis=1).astype(jnp.int32)
    pixel = jnp.arange(PB, dtype=jnp.int32)
    cycles = jnp.sum((pixel[None, :, None] >= ends[:, None, :]).astype(jnp.int32), axis=2)
    return cycles.reshape(-1).astype(jnp.int32)


def setup_inputs(seed: int = 0) -> dict:
    streams_of = jax.random.split(jax.random.key(seed), 3)
    frames = draw_frames(jax.random.fold_in(streams_of[2], 71), 0)
    cycle_map = draw_cycle_map(jax.random.fold_in(streams_of[2], 71), 0)
    return {"frames": frames, "cycle_map": cycle_map}


def reference(frames, cycle_map):
    onehot = cycle_map[:, None] == lax.iota(jnp.int32, CYCLES)[None, :]
    cycle_sums = jnp.dot(frames, onehot.astype(jnp.bfloat16), preferred_element_type=jnp.float32)
    counts = jnp.sum(onehot.astype(jnp.float32), axis=0)
    cycle_means = cycle_sums / counts[None, :]
    normalized = (frames.astype(jnp.float32) / cycle_means[:, cycle_map]).astype(jnp.bfloat16)
    wide = normalized.astype(jnp.float32)

    def per_cycle(cycle):
        masked = wide * (cycle_map == cycle).astype(jnp.float32)[None, :]
        gram = jnp.dot(masked, wide.T, precision=lax.Precision.HIGHEST)
        return gram / counts[cycle]

    return lax.map(per_cycle, jnp.arange(CYCLES, dtype=jnp.int32))
```

```python
import functools

import jax
import jax.numpy as jnp
from jax import lax
from jax.experimental import pallas as pl
from jax.experimental.pallas import tpu as pltpu
from jax.sharding import PartitionSpec as P

MESH = pl.DeviceIdType.MESH
CYCLES = 64
MAXP = 96
LANES = 128
SIDES, ROWS_Y, CORES = 2, 4, 2


def kernel(
    sizes, starts_ref, bases_ref, frames_ref, out_ref,
    packed, got, normed, scale, rows, part, theirs, mine, final,
    send1, recv1, send2, recv2, send3, recv3, send4, recv4,
):
    sides, ny, cores, nb, maxp = sizes
    block, pixels = frames_ref.shape
    own = out_ref.shape[0]
    width = own * maxp
    depth = rows.shape[1]
    ntm = sides * ny * cores
    tm = lax.axis_index("tm")
    band = lax.axis_index("band")
    side, y, core = tm // (ny * cores), (tm // cores) % ny, tm % cores

    barrier = pltpu.get_barrier_semaphore()

    def greet_band(k, _):
        pl.semaphore_signal(barrier, inc=1, device_id=(tm, (band + k) % nb), device_id_type=MESH)
        return 0

    def greet_tm(k, _):
        pl.semaphore_signal(barrier, inc=1, device_id=((tm + k) % ntm, band), device_id_type=MESH)
        return 0

    lax.fori_loop(1, nb, greet_band, 0)
    lax.fori_loop(1, ntm, greet_tm, 0)

    window = width + LANES
    lane = lax.broadcasted_iota(jnp.int32, (8, width), 1)
    pixel = lax.broadcasted_iota(jnp.int32, (window, width), 0)

    def pack(owner):
        base = bases_ref[owner]
        shift = jnp.full((block, LANES), base // LANES, jnp.int32)
        tiles = [frames_ref[:, LANES * t : LANES * (t + 1)] for t in range(pixels // LANES)]
        need = window // LANES
        for level in reversed(range((pixels // LANES - need).bit_length())):
            step = 1 << level
            moved = ((shift & step) > 0).astype(jnp.float32).astype(jnp.bfloat16) > 0
            tiles = [
                jnp.where(moved, tiles[t + step], tiles[t]) if t + step < len(tiles) else tiles[t]
                for t in range(min(len(tiles), step - 1 + need))
            ]
        view = jnp.concatenate(tiles[:need], axis=1)
        source = jnp.full((8, width), -1, jnp.int32)
        for j in range(own):
            start = starts_ref[owner * own + j]
            length = starts_ref[owner * own + j + 1] - start
            slot = lane - maxp * j
            source = jnp.where((slot >= 0) & (slot < length), slot + (start - base), source)
        onehot = jnp.where(pixel == source[:1], 1.0, 0.0).astype(jnp.bfloat16)
        picked = jnp.dot(view, onehot, preferred_element_type=jnp.float32)
        return picked.astype(jnp.bfloat16)

    got[band] = pack(band)
    pl.semaphore_wait(barrier, nb + ntm - 2)

    def send_band(k, _):
        owner = (band + k) % nb

        packed[owner] = pack(owner)
        pltpu.make_async_remote_copy(
            src_ref=packed.at[owner], dst_ref=got.at[band],
            send_sem=send1.at[owner], recv_sem=recv1.at[band],
            device_id=(tm, owner), device_id_type=MESH,
        ).start()
        return 0

    lax.fori_loop(1, nb, send_band, 0)

    def recv_band(k, _):
        source = (band + nb - k) % nb
        pltpu.make_async_remote_copy(
            src_ref=packed.at[source], dst_ref=got.at[source],
            send_sem=send1.at[source], recv_sem=recv1.at[source],
            device_id=(tm, source), device_id_type=MESH,
        ).wait_recv()
        return 0

    lax.fori_loop(1, nb, recv_band, 0)

    for j in range(own):
        wide = jnp.concatenate(
            [got[b, :, maxp * j : maxp * (j + 1)].astype(jnp.float32) for b in range(nb)], axis=1
        )
        total = jnp.sum(wide, axis=1, keepdims=True)
        count = jnp.sum((wide > 0).astype(jnp.float32), axis=1, keepdims=True)
        scale[j] = jnp.broadcast_to(1.0 / count, (block, LANES))
        normal = (wide * (count / total)).astype(jnp.bfloat16)
        for k in range(cores):
            normed[j, k] = normal[:, depth * k : depth * (k + 1)]

    def piece(index, sem):
        to_side, to_y, to_core = index // (ny * cores), (index // cores) % ny, index % cores
        return pltpu.make_async_remote_copy(
            src_ref=normed.at[to_y, to_core], dst_ref=rows.at[pl.ds(pl.multiple_of(sem * block, block), block)],
            send_sem=send2.at[index], recv_sem=recv2.at[sem],
            device_id=(index, band), device_id_type=MESH,
        )

    def send_tm(k, _):
        piece((tm + k) % ntm, tm).start()
        return 0

    lax.fori_loop(1, ntm, send_tm, 0)
    rows[pl.ds(pl.multiple_of(tm * block, block), block), :] = normed[y, core]

    def recv_tm(k, _):
        source = (tm + ntm - k) % ntm
        piece(source, source).wait_recv()
        return 0

    lax.fori_loop(1, ntm, recv_tm, 0)

    def gram(of_core):
        left = jnp.concatenate(
            [
                rows[pl.ds(pl.multiple_of(((side * ny + i) * cores + of_core) * block, block), block), :]
                for i in range(ny)
            ],
            axis=0,
        )
        return lax.dot_general(left, rows[...], (((1,), (1,)), ((), ())), preferred_element_type=jnp.float32)

    part[...] = gram(1 - core)
    pair = pltpu.make_async_remote_copy(
        src_ref=part, dst_ref=theirs, send_sem=send3, recv_sem=recv3,
        device_id=((side * ny + y) * cores + 1 - core, band), device_id_type=MESH,
    )
    pair.start()
    own_part = gram(core)
    pair.wait_recv()
    mine[...] = (own_part + theirs[...]).reshape(mine.shape)

    def result(i, slot):
        return pltpu.make_async_remote_copy(
            src_ref=mine.at[i], dst_ref=final.at[slot], send_sem=send4.at[i], recv_sem=recv4.at[slot],
            device_id=((side * ny + i) * cores + core, band), device_id_type=MESH,
        )

    def send_result(k, _):
        result((y + k) % ny, y).start()
        return 0

    lax.fori_loop(1, ny, send_result, 0)
    final[y] = mine[y]

    def recv_result(k, _):
        source = (y + ny - k) % ny
        result(source, source).wait_recv()
        return 0

    lax.fori_loop(1, ny, recv_result, 0)
    for j in range(own):
        out_ref[j] = final[j] * scale[j, :, :1]

    def drain_band(k, _):
        owner = (band + k) % nb
        pltpu.make_async_remote_copy(
            src_ref=packed.at[owner], dst_ref=got.at[band],
            send_sem=send1.at[owner], recv_sem=recv1.at[band],
            device_id=(tm, owner), device_id_type=MESH,
        ).wait_send()
        return 0

    def drain_tm(k, _):
        piece((tm + k) % ntm, tm).wait_send()
        return 0

    def drain_result(k, _):
        result((y + k) % ny, y).wait_send()
        return 0

    lax.fori_loop(1, nb, drain_band, 0)
    lax.fori_loop(1, ntm, drain_tm, 0)
    pair.wait_send()
    lax.fori_loop(1, ny, drain_result, 0)


def local(sizes, cycles, frames, cycle_map):
    sides, ny, cores, nb, maxp = sizes
    block = frames.shape[0]
    ntm = sides * ny * cores
    own = cycles // nb
    width, depth = own * maxp, nb * maxp // cores
    starts = jnp.sum(
        (cycle_map[None, :] < lax.iota(jnp.int32, cycles + 1)[:, None]).astype(jnp.int32), axis=1
    )
    bases = jnp.minimum(starts[:-1:own] // LANES * LANES, frames.shape[1] - width - LANES)
    dma = pltpu.SemaphoreType.DMA
    return pl.pallas_call(
        functools.partial(kernel, sizes),
        out_shape=jax.ShapeDtypeStruct((own, block, ntm * block), jnp.float32),
        in_specs=[pl.BlockSpec(memory_space=pltpu.SMEM)] * 2 + [pl.BlockSpec(memory_space=pltpu.VMEM)],
        out_specs=pl.BlockSpec(memory_space=pltpu.VMEM),
        scratch_shapes=[
            pltpu.VMEM((nb, block, width), jnp.bfloat16),
            pltpu.VMEM((nb, block, width), jnp.bfloat16),
            pltpu.VMEM((own, cores, block, depth), jnp.bfloat16),
            pltpu.VMEM((own, block, LANES), jnp.float32),
            pltpu.VMEM((ntm * block, depth), jnp.bfloat16),
            pltpu.VMEM((ny * block, ntm * block), jnp.float32),
            pltpu.VMEM((ny * block, ntm * block), jnp.float32),
            pltpu.VMEM((ny, block, ntm * block), jnp.float32),
            pltpu.VMEM((ny, block, ntm * block), jnp.float32),
            dma((nb,)), dma((nb,)), dma((ntm,)), dma((ntm,)), dma, dma, dma((ny,)), dma((ny,)),
        ],
        compiler_params=pltpu.CompilerParams(
            collective_id=0, has_side_effects=True, vmem_limit_bytes=32 * 1024 * 1024
        ),
    )(starts, bases, frames)


def solution(mesh):
    return jax.shard_map(
        functools.partial(local, (SIDES, ROWS_Y, CORES, mesh.shape["band"], MAXP), CYCLES),
        mesh=mesh,
        in_specs=(P("tm", "band"), P("band")),
        out_specs=P("band", "tm", None),
        check_vma=False,
    )
```

```python
import functools

import jax
import jax.numpy as jnp
from jax import lax
from jax.experimental import pallas as pl
from jax.experimental.pallas import tpu as pltpu
from jax.sharding import PartitionSpec as P

MESH = pl.DeviceIdType.MESH
CYCLES = 64
MAXP = 96
LANES = 128
SIDES, ROWS_Y, CORES = 2, 4, 2
HALVES = 2


def kernel(
    sizes, frames_hbm, map_hbm, out_ref,
    frames_ref, map_ref, source_ref, shift_ref,
    packed, got, normed, scale, rows, part, theirs, mine, final,
    load_sem, send1, recv1, send2, recv2, send3, recv3, send4, recv4,
):
    sides, ny, cores, nb, maxp = sizes
    block, pixels = frames_ref.shape
    own = out_ref.shape[0]
    width = own * maxp
    depth = rows.shape[1]
    ring = ny * cores
    sub = block // HALVES
    window = width + LANES
    ntile = pixels // LANES
    need = window // LANES
    tm = lax.axis_index("tm")
    band = lax.axis_index("band")
    side, place, core = tm // ring, tm % ring, tm % cores
    y = place // cores
    far = sides - 1 - side
    major = (y % sides) == side

    load_map = pltpu.make_async_copy(map_hbm, map_ref, load_sem.at[0])
    load_frames = pltpu.make_async_copy(frames_hbm, frames_ref, load_sem.at[1])
    load_map.start()
    load_frames.start()

    barrier = pltpu.get_barrier_semaphore()

    def loop(low, high, body):
        def step(k, carry):
            body(k)
            return carry

        lax.fori_loop(low, high, step, 0)

    def greet(to_tm, to_band):
        pl.semaphore_signal(barrier, inc=1, device_id=(to_tm, to_band), device_id_type=MESH)

    loop(1, nb, lambda k: greet(tm, (band + k) % nb))
    loop(1, sides * ring, lambda k: greet((tm + k) % (sides * ring), band))

    load_map.wait()
    first = own * lax.broadcasted_iota(jnp.int32, (nb, LANES), 0)
    starts = []
    for j in range(own + 1):
        below = jnp.zeros((nb, LANES), jnp.int32)
        for t in range(ntile):
            below += jnp.where(map_ref[t : t + 1, :] < first + j, 1, 0)
        starts.append(jnp.sum(below.astype(jnp.float32), axis=1, keepdims=True).astype(jnp.int32))
    tile = jnp.minimum(starts[0] // LANES, ntile - need)
    lane = lax.broadcasted_iota(jnp.int32, (nb, width), 1)
    source = jnp.full((nb, width), -1, jnp.int32)
    for j in range(own):
        slot = lane - maxp * j
        inside = (slot >= 0) & (slot < starts[j + 1] - starts[j])
        source = jnp.where(inside, slot + (starts[j] - LANES * tile), source)
    source_ref[...] = source
    shift_ref[...] = jnp.broadcast_to(tile, (nb, LANES))
    load_frames.wait()

    pixel = lax.broadcasted_iota(jnp.int32, (window, width), 0)

    def pack(owner):
        shift = jnp.broadcast_to(shift_ref[pl.ds(owner, 1), :], (block, LANES))
        tiles = [frames_ref[:, LANES * t : LANES * (t + 1)] for t in range(ntile)]
        for level in reversed(range((ntile - need).bit_length())):
            step = 1 << level
            moved = ((shift & step) > 0).astype(jnp.float32).astype(jnp.bfloat16) > 0
            tiles = [
                jnp.where(moved, tiles[t + step], tiles[t]) if t + step < len(tiles) else tiles[t]
                for t in range(min(len(tiles), step - 1 + need))
            ]
        view = jnp.concatenate(tiles[:need], axis=1)
        onehot = jnp.where(pixel == source_ref[pl.ds(owner, 1), :], 1.0, 0.0).astype(jnp.bfloat16)
        return jnp.dot(view, onehot, preferred_element_type=jnp.float32).astype(jnp.bfloat16)

    def chunk(half, owner, slot):
        lines = pl.ds(half * sub, sub)
        return pltpu.make_async_remote_copy(
            src_ref=packed.at[owner, lines], dst_ref=got.at[slot, lines],
            send_sem=send1.at[half, owner], recv_sem=recv1.at[half, slot],
            device_id=(tm, owner), device_id_type=MESH,
        )

    def piece(half, to_side, to, slot):
        return pltpu.make_async_remote_copy(
            src_ref=normed.at[to // cores, to % cores, pl.ds(half * sub, sub)],
            dst_ref=rows.at[pl.ds(pl.multiple_of(slot * block + half * sub, sub), sub)],
            send_sem=send2.at[half, to_side, to], recv_sem=recv2.at[half, slot],
            device_id=(to_side * ring + to, band), device_id_type=MESH,
        )

    far_places = [(sides * i + far) * cores + k for i in range(ny // sides) for k in range(cores)] if sides > 1 else []

    def spread(half):
        lines = slice(half * sub, (half + 1) * sub)
        for j in range(own):
            wide = jnp.concatenate(
                [got[b, lines, maxp * j : maxp * (j + 1)].astype(jnp.float32) for b in range(nb)], axis=1
            )
            total = jnp.sum(wide, axis=1, keepdims=True)
            count = jnp.sum((wide > 0).astype(jnp.float32), axis=1, keepdims=True)
            scale[j, lines] = jnp.broadcast_to(1.0 / count, (sub, LANES))
            normal = (wide * (count / total)).astype(jnp.bfloat16)
            for k in range(cores):
                normed[j, k, lines] = normal[:, depth * k : depth * (k + 1)]
        for to in far_places:
            piece(half, far, to, tm).start()
        loop(1, ring, lambda k: piece(half, side, (place + k) % ring, tm).start())
        rows[pl.ds(pl.multiple_of(tm * block + half * sub, sub), sub), :] = normed[y, core, lines]

    got[band] = pack(band)
    pl.semaphore_wait(barrier, nb + sides * ring - 2)

    def send_first(k):
        owner = (band + k) % nb
        packed[owner] = pack(owner)
        chunk(0, owner, band).start()

    loop(1, nb, send_first)
    for half in range(1, HALVES):

        def send_next(k):
            chunk(half - 1, (band + k) % nb, (band + nb - k) % nb).wait_recv()
            chunk(half, (band + k) % nb, band).start()

        loop(1, nb, send_next)
        spread(half - 1)

    loop(1, nb, lambda k: chunk(HALVES - 1, (band + k) % nb, (band + nb - k) % nb).wait_recv())
    spread(HALVES - 1)
    for half in range(HALVES):
        loop(1, ring, lambda k: piece(half, side, (place + k) % ring, side * ring + (place + ring - k) % ring).wait_recv())
        if sides > 1:

            @pl.when(major)
            def _():
                loop(0, ring, lambda k: piece(half, side, k, far * ring + k).wait_recv())

    def gram(kind, of_core):
        left_side = far if kind == 2 else side
        right_side = far if kind == 1 else side
        left = jnp.concatenate(
            [
                rows[pl.ds(pl.multiple_of((left_side * ring + i * cores + of_core) * block, block), block), :]
                for i in range(ny)
            ],
            axis=0,
        )
        right = rows[pl.ds(pl.multiple_of(right_side * ring * block, ring * block), ring * block), :]
        return lax.dot_general(left, right, (((1,), (1,)), ((), ())), preferred_element_type=jnp.float32)

    def pair(kind):
        return pltpu.make_async_remote_copy(
            src_ref=part.at[kind], dst_ref=theirs.at[kind], send_sem=send3.at[kind], recv_sem=recv3.at[kind],
            device_id=(side * ring + y * cores + 1 - core, band), device_id_type=MESH,
        )

    def result(kind, i, slot, columns):
        return pltpu.make_async_remote_copy(
            src_ref=mine.at[kind, i], dst_ref=final.at[slot, columns],
            send_sem=send4.at[kind, i], recv_sem=recv4.at[slot, columns],
            device_id=((far if kind == 2 else side) * ring + i * cores + core, band), device_id_type=MESH,
        )

    def give(kind):
        part[kind] = gram(kind, 1 - core)
        pair(kind).start()

    def take(kind):
        own_part = gram(kind, core)
        pair(kind).wait_recv()
        mine[kind] = (own_part + theirs[kind]).reshape(mine.shape[1:])
        if kind == 2:
            loop(0, ny, lambda k: result(2, (y + k) % ny, y, side).start())
        else:
            columns = side if kind == 0 else far
            loop(1, ny, lambda k: result(kind, (y + k) % ny, y, columns).start())
            final[y, columns] = mine[kind, y]

    give(0)
    if sides > 1:

        @pl.when(major)
        def _():
            give(2)
            give(1)
            take(2)
            take(1)

    take(0)

    for columns in range(sides):
        loop(1, ny, lambda k: result(0, (y + k) % ny, (y + ny - k) % ny, columns).wait_recv())
    if sides > 1:

        @pl.when(jnp.logical_not(major))
        def _():
            result(0, y, y, far).wait_recv()

    for j in range(own):
        for columns in range(sides):
            out_ref[j, :, ring * block * columns : ring * block * (columns + 1)] = final[j, columns] * scale[j, :, :1]

    for half in range(HALVES):
        loop(1, nb, lambda k: chunk(half, (band + k) % nb, band).wait_send())
        loop(1, ring, lambda k: piece(half, side, (place + k) % ring, tm).wait_send())
        for to in far_places:
            piece(half, far, to, tm).wait_send()
    pair(0).wait_send()
    loop(1, ny, lambda k: result(0, (y + k) % ny, y, side).wait_send())
    if sides > 1:

        @pl.when(major)
        def _():
            pair(1).wait_send()
            pair(2).wait_send()
            loop(1, ny, lambda k: result(1, (y + k) % ny, y, far).wait_send())
            loop(0, ny, lambda k: result(2, (y + k) % ny, y, side).wait_send())


def local(sizes, cycles, frames, cycle_map):
    sides, ny, cores, nb, maxp = sizes
    block, pixels = frames.shape
    ring = ny * cores
    ntm = sides * ring
    own = cycles // nb
    width, depth = own * maxp, nb * maxp // cores
    dma = pltpu.SemaphoreType.DMA
    return pl.pallas_call(
        functools.partial(kernel, sizes),
        out_shape=jax.ShapeDtypeStruct((own, block, ntm * block), jnp.float32),
        in_specs=[pl.BlockSpec(memory_space=pltpu.HBM)] * 2,
        out_specs=pl.BlockSpec(memory_space=pltpu.VMEM),
        scratch_shapes=[
            pltpu.VMEM((block, pixels), jnp.bfloat16),
            pltpu.VMEM((pixels // LANES, LANES), jnp.int32),
            pltpu.VMEM((nb, width), jnp.int32),
            pltpu.VMEM((nb, LANES), jnp.int32),
            pltpu.VMEM((nb, block, width), jnp.bfloat16),
            pltpu.VMEM((nb, block, width), jnp.bfloat16),
            pltpu.VMEM((own, cores, block, depth), jnp.bfloat16),
            pltpu.VMEM((own, block, LANES), jnp.float32),
            pltpu.VMEM((ntm * block, depth), jnp.bfloat16),
            pltpu.VMEM((3, ny * block, ring * block), jnp.float32),
            pltpu.VMEM((3, ny * block, ring * block), jnp.float32),
            pltpu.VMEM((3, ny, block, ring * block), jnp.float32),
            pltpu.VMEM((ny, sides, block, ring * block), jnp.float32),
            dma((2,)), dma((HALVES, nb)), dma((HALVES, nb)), dma((HALVES, sides, ring)), dma((HALVES, ntm)),
            dma((3,)), dma((3,)), dma((3, ny)), dma((ny, sides)),
        ],
        compiler_params=pltpu.CompilerParams(
            collective_id=0, has_side_effects=True, vmem_limit_bytes=32 * 1024 * 1024
        ),
    )(frames, cycle_map.reshape(pixels // LANES, LANES))


def solution(mesh):
    return jax.shard_map(
        functools.partial(local, (SIDES, ROWS_Y, CORES, mesh.shape["band"], MAXP), CYCLES),
        mesh=mesh,
        in_specs=(P("tm", "band"), P("band")),
        out_specs=P("band", "tm", None),
        check_vma=False,
    )
```

```python
import functools

import jax
import jax.numpy as jnp
from jax import lax
from jax.experimental import pallas as pl
from jax.experimental.pallas import tpu as pltpu
from jax.sharding import PartitionSpec as P

MESH = pl.DeviceIdType.MESH
CYCLES = 64
MAXP = 96
LANES = 128
SIDES, ROWS_Y, CORES = 2, 4, 2
HALVES = 2
EARLY = 8
VMEM_LIMIT = 107 * 512 * 1024


def kernel(
    sizes, frames_hbm, map_hbm, out_ref,
    frames_ref, map_ref, source_ref, shift_ref,
    packed, got, normed, scale, rows, blocks, theirs, mine, final,
    load_sem, send1, recv1, send2, recv2, send3, recv3, send4, recv4,
):
    sides, ny, cores, nb, maxp = sizes
    block, pixels = frames_ref.shape
    own = out_ref.shape[0]
    width = own * maxp
    depth = rows.shape[1]
    ring = ny * cores
    sub = block // HALVES
    window = width + LANES
    ntile = pixels // LANES
    need = window // LANES
    tm = lax.axis_index("tm")
    band = lax.axis_index("band")
    side, place, core = lax.div(tm, ring), lax.rem(tm, ring), lax.rem(tm, cores)
    y = lax.div(place, cores)
    far = sides - 1 - side
    major = lax.rem(y, sides) == side

    load_map = pltpu.make_async_copy(map_hbm, map_ref, load_sem.at[0])
    load_frames = pltpu.make_async_copy(frames_hbm, frames_ref, load_sem.at[1])
    load_map.start()
    load_frames.start()

    barrier = pltpu.get_barrier_semaphore()

    def loop(low, high, body):
        for k in range(low, high):
            body(k)

    def after(k):
        return lax.rem(band + k, nb)

    def beyond(k):
        return lax.rem(y + [0, ny // 2, 1, ny - 1][k], ny)

    def next_to(k):
        if k < 2 * ny - 1:
            return beyond(1 + (k - 1) // cores) * cores + (k - 1) % cores
        return y * cores + 1 - core

    def arrived(ref, sem):
        pltpu.make_async_copy(ref, ref, sem).wait()

    def greet(to_tm, to_band):
        pl.semaphore_signal(barrier, inc=1, device_id=(to_tm, to_band), device_id_type=MESH)

    loop(1, nb, lambda k: greet(tm, after(k)))
    loop(1, sides * ring, lambda k: greet(lax.rem(tm + k, sides * ring), band))

    load_map.wait()
    first = own * lax.broadcasted_iota(jnp.int32, (nb, LANES), 0)
    starts = []
    for j in range(own + 1):
        below = jnp.zeros((nb, LANES), jnp.int32)
        for t in range(ntile):
            below += jnp.where(map_ref[t : t + 1, :] < first + j, 1, 0)
        starts.append(jnp.sum(below.astype(jnp.float32), axis=1, keepdims=True).astype(jnp.int32))
    tile = jnp.minimum(starts[0] // LANES, ntile - need)
    lane = lax.broadcasted_iota(jnp.int32, (nb, width), 1)
    source = jnp.full((nb, width), -1, jnp.int32)
    for j in range(own):
        slot = lane - maxp * j
        inside = (slot >= 0) & (slot < starts[j + 1] - starts[j])
        source = jnp.where(inside, slot + (starts[j] - LANES * tile), source)
    source_ref[...] = source
    shift_ref[...] = jnp.broadcast_to(tile, (nb, LANES))
    load_frames.wait()

    pixel = lax.broadcasted_iota(jnp.int32, (window, width), 0)

    def pack(owner):
        shift = jnp.broadcast_to(shift_ref[pl.ds(owner, 1), :], (block, LANES))
        tiles = [frames_ref[:, LANES * t : LANES * (t + 1)] for t in range(ntile)]
        for level in reversed(range((ntile - need).bit_length())):
            step = 1 << level
            moved = ((shift & step) > 0).astype(jnp.float32).astype(jnp.bfloat16) > 0
            tiles = [
                jnp.where(moved, tiles[t + step], tiles[t]) if t + step < len(tiles) else tiles[t]
                for t in range(min(len(tiles), step - 1 + need))
            ]
        view = jnp.concatenate(tiles[:need], axis=1)
        onehot = jnp.where(pixel == source_ref[pl.ds(owner, 1), :], 1.0, 0.0).astype(jnp.bfloat16)
        return jnp.dot(view, onehot, preferred_element_type=jnp.float32).astype(jnp.bfloat16)

    def chunk(half, owner, slot):
        lines = pl.ds(half * sub, sub)
        return pltpu.make_async_remote_copy(
            src_ref=packed.at[owner, lines], dst_ref=got.at[slot, lines],
            send_sem=send1, recv_sem=recv1.at[half],
            device_id=(tm, owner), device_id_type=MESH,
        )

    def piece(half, to_side, to, slot):
        return pltpu.make_async_remote_copy(
            src_ref=normed.at[to // cores, to % cores, pl.ds(half * sub, sub)],
            dst_ref=rows.at[pl.ds(pl.multiple_of(slot * block + half * sub, sub), sub)],
            send_sem=send2, recv_sem=recv2.at[0 if to_side is side else 1],
            device_id=(to_side * ring + to, band), device_id_type=MESH,
        )

    far_places = [(sides * i + far) * cores + k for i in range(ny // sides) for k in range(cores)] if sides > 1 else []

    def spread(half):
        lines = slice(half * sub, (half + 1) * sub)
        for j in range(own):
            wide = jnp.concatenate(
                [got[b, lines, maxp * j : maxp * (j + 1)].astype(jnp.float32) for b in range(nb)], axis=1
            )
            total = jnp.sum(wide, axis=1, keepdims=True)
            count = jnp.sum((wide > 0).astype(jnp.float32), axis=1, keepdims=True)
            scale[j, lines] = jnp.broadcast_to(1.0 / count, (sub, LANES))
            normal = (wide * (count / total)).astype(jnp.bfloat16)
            for k in range(cores):
                normed[j, k, lines] = normal[:, depth * k : depth * (k + 1)]
        for to in far_places:
            piece(half, far, to, tm).start()
        loop(1, ring, lambda k: piece(half, side, next_to(k), tm).start())
        rows[pl.ds(pl.multiple_of(tm * block + half * sub, sub), sub), :] = normed[y, core, lines]

    def prepare(k, carry):
        packed[after(k)] = pack(after(k))
        return carry

    def send_first(k, carry):
        chunk(0, after(k), band).start()
        return carry

    def prepare_and_send(k, carry):
        prepare(k, carry)
        return send_first(k, carry)

    early = min(EARLY, nb - 1)
    lax.fori_loop(1, early + 1, prepare, 0)
    pl.semaphore_wait(barrier, nb + sides * ring - 2)
    lax.fori_loop(1, early + 1, send_first, 0)
    lax.fori_loop(early + 1, nb, prepare_and_send, 0)
    got[band] = pack(band)
    for half in range(HALVES):
        if half + 1 < HALVES:
            loop(1, nb, lambda k: chunk(half + 1, after(k), band).start())
        arrived(got.at[pl.ds(0, nb - 1), pl.ds(0, sub)], recv1.at[half])
        spread(half)

    def gram(kind):
        side_of = lambda other: pl.ds(pl.multiple_of((far if other else side) * ring * block, ring * block), ring * block)
        blocks[kind] = lax.dot_general(
            rows[side_of(kind == 2), :], rows[side_of(kind == 1), :], (((1,), (1,)), ((), ())),
            preferred_element_type=jnp.float32,
        ).reshape(blocks.shape[1:])
        pair(kind).start()

    def pair(kind):
        return pltpu.make_async_remote_copy(
            src_ref=blocks.at[kind, pl.ds(0, ny), 1 - core], dst_ref=theirs.at[kind],
            send_sem=send3.at[kind], recv_sem=recv3.at[kind],
            device_id=(side * ring + y * cores + 1 - core, band), device_id_type=MESH,
        )

    def result(kind, i, slot, columns):
        return pltpu.make_async_remote_copy(
            src_ref=mine.at[kind * ny + i], dst_ref=final.at[slot * sides + columns], send_sem=send4, recv_sem=recv4,
            device_id=((far if kind == 2 else side) * ring + i * cores + core, band), device_id_type=MESH,
        )

    def finish(kind):
        pair(kind).wait_recv()
        mine[ny * kind : ny * (kind + 1)] = blocks[kind, :, core] + theirs[kind]
        if kind == 2:
            loop(0, ny, lambda k: result(2, beyond((k + 1) % ny), y, side).start())
        else:
            columns = side if kind == 0 else far
            loop(1, ny, lambda k: result(kind, beyond(k), y, columns).start())
            final[y * sides + columns] = mine[ny * kind + y]

    arrived(rows.at[pl.ds(0, (ring - 1) * block)], recv2.at[0])
    gram(0)
    if sides > 1:

        @pl.when(major)
        def _():
            arrived(rows.at[pl.ds(0, ring * block)], recv2.at[1])
            gram(2)
            gram(1)
            finish(2)
            finish(1)

    finish(0)

    if sides > 1:

        @pl.when(major)
        def _():
            arrived(final.at[pl.ds(0, (ny - 1) * sides)], recv4)

        @pl.when(jnp.logical_not(major))
        def _():
            arrived(final.at[pl.ds(0, ny * sides - 1)], recv4)

    else:
        arrived(final.at[pl.ds(0, ny - 1)], recv4)

    for j in range(own):
        for columns in range(sides):
            out_ref[j, :, ring * block * columns : ring * block * (columns + 1)] = final[sides * j + columns] * scale[j, :, :1]

    arrived(packed.at[pl.ds(0, nb - 1)], send1)
    arrived(rows.at[pl.ds(0, (ring - 1 + len(far_places)) * block)], send2)
    pair(0).wait_send()
    if sides > 1:

        @pl.when(major)
        def _():
            pair(1).wait_send()
            pair(2).wait_send()
            arrived(mine.at[pl.ds(0, 3 * ny - 2)], send4)

        @pl.when(jnp.logical_not(major))
        def _():
            arrived(mine.at[pl.ds(0, ny - 1)], send4)

    else:
        arrived(mine.at[pl.ds(0, ny - 1)], send4)


def local(sizes, cycles, frames, cycle_map):
    sides, ny, cores, nb, maxp = sizes
    block, pixels = frames.shape
    ring = ny * cores
    ntm = sides * ring
    own = cycles // nb
    width, depth = own * maxp, nb * maxp // cores
    dma = pltpu.SemaphoreType.DMA
    return pl.pallas_call(
        functools.partial(kernel, sizes),
        out_shape=jax.ShapeDtypeStruct((own, block, ntm * block), jnp.float32),
        in_specs=[pl.BlockSpec(memory_space=pltpu.HBM)] * 2,
        out_specs=pl.BlockSpec(memory_space=pltpu.VMEM),
        scratch_shapes=[
            pltpu.VMEM((block, pixels), jnp.bfloat16),
            pltpu.VMEM((pixels // LANES, LANES), jnp.int32),
            pltpu.VMEM((nb, width), jnp.int32),
            pltpu.VMEM((nb, LANES), jnp.int32),
            pltpu.VMEM((nb, block, width), jnp.bfloat16),
            pltpu.VMEM((nb, block, width), jnp.bfloat16),
            pltpu.VMEM((own, cores, block, depth), jnp.bfloat16),
            pltpu.VMEM((own, block, LANES), jnp.float32),
            pltpu.VMEM((ntm * block, depth), jnp.bfloat16),
            pltpu.VMEM((3, ny, cores, block, ring * block), jnp.float32),
            pltpu.VMEM((3, ny, block, ring * block), jnp.float32),
            pltpu.VMEM((3 * ny, block, ring * block), jnp.float32),
            pltpu.VMEM((ny * sides, block, ring * block), jnp.float32),
            dma((2,)), dma, dma((HALVES,)), dma, dma((2,)), dma((3,)), dma((3,)), dma, dma,
        ],
        compiler_params=pltpu.CompilerParams(
            collective_id=0, has_side_effects=True, vmem_limit_bytes=VMEM_LIMIT
        ),
    )(frames, cycle_map.reshape(pixels // LANES, LANES))


def solution(mesh):
    return jax.shard_map(
        functools.partial(local, (SIDES, ROWS_Y, CORES, mesh.shape["band"], MAXP), CYCLES),
        mesh=mesh,
        in_specs=(P("tm", "band"), P("band")),
        out_specs=P("band", "tm", None),
        check_vma=False,
    )
```

```python
import functools

import jax
import jax.numpy as jnp
from jax import lax
from jax.experimental import pallas as pl
from jax.experimental.pallas import tpu as pltpu
from jax.sharding import PartitionSpec as P

MESH = pl.DeviceIdType.MESH
CYCLES = 64
MAXP = 96
LANES = 128
SIDES, ROWS_Y, CORES = 2, 4, 2
HALVES = 2
EARLY = 8
VMEM_LIMIT = 107 * 512 * 1024


def kernel(
    sizes, frames_hbm, map_hbm, out_ref,
    frames_ref, map_ref, source_ref, shift_ref,
    packed, got, normed, scale, rows, blocks, theirs, mine, final,
    load_sem, send1, recv1, send2, recv2, send3, recv3, send4, recv4,
):
    sides, ny, cores, nb, maxp = sizes
    block, pixels = frames_ref.shape
    own = out_ref.shape[0]
    width = own * maxp
    depth = rows.shape[1]
    ring = ny * cores
    sub = block // HALVES
    window = width + LANES
    ntile = pixels // LANES
    need = window // LANES
    tm = lax.axis_index("tm")
    band = lax.axis_index("band")
    side, place, core = lax.div(tm, ring), lax.rem(tm, ring), lax.rem(tm, cores)
    y = lax.div(place, cores)
    far = sides - 1 - side
    major = lax.rem(y, sides) == side

    turns = ([2, 3, 1, 0] if ny == 4 else list(range(ny - 1, -1, -1)))
    lead = (own + 1) // 2
    split = min(-(-lead * maxp // LANES) * LANES, width)
    parts = [(0, 0, width), (1, 0, split)] + ([(1, split, width)] if split < width else [])

    def at_turn(i):
        return lax.rem(y + turns[i], ny)

    load_map = pltpu.make_async_copy(map_hbm, map_ref, load_sem.at[0])
    load_frames = pltpu.make_async_copy(frames_hbm, frames_ref, load_sem.at[1])
    load_map.start()
    load_frames.start()

    barrier = pltpu.get_barrier_semaphore()

    def loop(low, high, body):
        for k in range(low, high):
            body(k)

    def after(k):
        return lax.rem(band + k, nb)

    def beyond(k):
        return lax.rem(y + [0, ny // 2, 1, ny - 1][k], ny)

    def arrived(ref, sem):
        pltpu.make_async_copy(ref, ref, sem).wait()

    def greet(to_tm, to_band):
        pl.semaphore_signal(barrier, inc=1, device_id=(to_tm, to_band), device_id_type=MESH)

    loop(1, nb, lambda k: greet(tm, after(k)))
    loop(1, sides * ring, lambda k: greet(lax.rem(tm + k, sides * ring), band))

    load_map.wait()
    first = own * lax.broadcasted_iota(jnp.int32, (nb, LANES), 0)

    def pixels_below(cycle):
        below = jnp.zeros((nb, LANES), jnp.int32)
        for t in range(ntile):
            below += jnp.where(map_ref[t : t + 1, :] < first + cycle, 1, 0)
        return jnp.sum(below.astype(jnp.float32), axis=1, keepdims=True).astype(jnp.int32)

    tile = jnp.minimum(pixels_below(0) // LANES, ntile - need)
    lane = lax.broadcasted_iota(jnp.int32, (nb, width), 1)
    source = jnp.full((nb, width), -1, jnp.int32)
    for j in range(own):
        slot = lane - maxp * j
        start = pixels_below(at_turn(j))
        inside = (slot >= 0) & (slot < pixels_below(at_turn(j) + 1) - start)
        source = jnp.where(inside, slot + (start - LANES * tile), source)
    source_ref[...] = source
    shift_ref[...] = jnp.broadcast_to(tile, (nb, LANES))
    load_frames.wait()

    pixel = lax.broadcasted_iota(jnp.int32, (window, width), 0)

    def pack(owner):
        shift = jnp.broadcast_to(shift_ref[pl.ds(owner, 1), :], (block, LANES))
        tiles = [frames_ref[:, LANES * t : LANES * (t + 1)] for t in range(ntile)]
        for level in reversed(range((ntile - need).bit_length())):
            step = 1 << level
            moved = ((shift & step) > 0).astype(jnp.float32).astype(jnp.bfloat16) > 0
            tiles = [
                jnp.where(moved, tiles[t + step], tiles[t]) if t + step < len(tiles) else tiles[t]
                for t in range(min(len(tiles), step - 1 + need))
            ]
        view = jnp.concatenate(tiles[:need], axis=1)
        onehot = jnp.where(pixel == source_ref[pl.ds(owner, 1), :], 1.0, 0.0).astype(jnp.bfloat16)
        return jnp.dot(view, onehot, preferred_element_type=jnp.float32).astype(jnp.bfloat16)

    def chunk(part, owner):
        half, low, high = parts[part]
        lines = pl.ds(half * sub, sub)
        return pltpu.make_async_remote_copy(
            src_ref=packed.at[owner, lines, pl.ds(low, high - low)], dst_ref=got.at[band, lines, pl.ds(low, high - low)],
            send_sem=send1, recv_sem=recv1.at[part], device_id=(tm, owner), device_id_type=MESH,
        )

    def piece(half, to_side, to, slot):
        return pltpu.make_async_remote_copy(
            src_ref=normed.at[to // cores, to % cores, pl.ds(half * sub, sub)],
            dst_ref=rows.at[pl.ds(pl.multiple_of(slot * block + half * sub, sub), sub)],
            send_sem=send2, recv_sem=recv2.at[0 if to_side is side else 1],
            device_id=(to_side * ring + to, band), device_id_type=MESH,
        )

    def spread(half, slots):
        lines = slice(half * sub, (half + 1) * sub)
        for i in slots:
            wide = jnp.concatenate(
                [got[b, lines, maxp * i : maxp * (i + 1)].astype(jnp.float32) for b in range(nb)], axis=1
            )
            total = jnp.sum(wide, axis=1, keepdims=True)
            count = jnp.sum((wide > 0).astype(jnp.float32), axis=1, keepdims=True)
            scale[at_turn(i), lines] = jnp.broadcast_to(1.0 / count, (sub, LANES))
            normal = (wide * (count / total)).astype(jnp.bfloat16)
            for k in range(cores):
                normed[at_turn(i), k, lines] = normal[:, depth * k : depth * (k + 1)]
        for i in slots:
            to = at_turn(i) * cores
            if sides > 1:

                @pl.when(lax.rem(at_turn(i), sides) == far)
                def _():
                    for k in range(cores):
                        piece(half, far, to + k, tm).start()

            if turns[i]:
                for k in range(cores):
                    piece(half, side, to + k, tm).start()
            else:
                piece(half, side, to + 1 - core, tm).start()
                rows[pl.ds(pl.multiple_of(tm * block + half * sub, sub), sub), :] = normed[y, core, lines]

    def prepare(k, carry):
        packed[after(k)] = pack(after(k))
        return carry

    def send_first(k, carry):
        chunk(0, after(k)).start()
        return carry

    def prepare_and_send(k, carry):
        prepare(k, carry)
        return send_first(k, carry)

    early = min(EARLY, nb - 1)
    lax.fori_loop(1, early + 1, prepare, 0)
    pl.semaphore_wait(barrier, nb + sides * ring - 2)
    lax.fori_loop(1, early + 1, send_first, 0)
    lax.fori_loop(early + 1, nb, prepare_and_send, 0)
    got[band] = pack(band)
    for part in range(1, len(parts)):
        loop(1, nb, lambda k: chunk(part, after(k)).start())
    for part, (half, low, high) in enumerate(parts):
        arrived(got.at[pl.ds(0, nb - 1), pl.ds(0, sub), pl.ds(low, high - low)], recv1.at[part])
        if part == 0:
            spread(0, range(own))
        elif part == 1:
            spread(1, range(lead))
    spread(1, range(lead, own))

    def gram(kind):
        side_of = lambda other: pl.ds(pl.multiple_of((far if other else side) * ring * block, ring * block), ring * block)
        blocks[kind] = lax.dot_general(
            rows[side_of(kind == 2), :], rows[side_of(kind == 1), :], (((1,), (1,)), ((), ())),
            preferred_element_type=jnp.float32,
        ).reshape(blocks.shape[1:])
        pair(kind).start()

    def pair(kind):
        return pltpu.make_async_remote_copy(
            src_ref=blocks.at[kind, pl.ds(0, ny), 1 - core], dst_ref=theirs.at[kind],
            send_sem=send3.at[kind], recv_sem=recv3.at[kind],
            device_id=(side * ring + y * cores + 1 - core, band), device_id_type=MESH,
        )

    def result(kind, i, slot, columns):
        return pltpu.make_async_remote_copy(
            src_ref=mine.at[kind * ny + i], dst_ref=final.at[slot * sides + columns], send_sem=send4, recv_sem=recv4,
            device_id=((far if kind == 2 else side) * ring + i * cores + core, band), device_id_type=MESH,
        )

    def finish(kind):
        pair(kind).wait_recv()
        mine[ny * kind : ny * (kind + 1)] = blocks[kind, :, core] + theirs[kind]
        if kind == 2:
            loop(0, ny, lambda k: result(2, beyond((k + 1) % ny), y, side).start())
        else:
            columns = side if kind == 0 else far
            loop(1, ny, lambda k: result(kind, beyond(k), y, columns).start())
            final[y * sides + columns] = mine[ny * kind + y]

    arrived(rows.at[pl.ds(0, (ring - 1) * block)], recv2.at[0])
    gram(0)
    if sides > 1:

        @pl.when(major)
        def _():
            arrived(rows.at[pl.ds(0, ring * block)], recv2.at[1])
            gram(2)
            gram(1)
            finish(2)
            finish(1)

    finish(0)

    if sides > 1:

        @pl.when(major)
        def _():
            arrived(final.at[pl.ds(0, (ny - 1) * sides)], recv4)

        @pl.when(jnp.logical_not(major))
        def _():
            arrived(final.at[pl.ds(0, ny * sides - 1)], recv4)

    else:
        arrived(final.at[pl.ds(0, ny - 1)], recv4)

    for j in range(own):
        for columns in range(sides):
            out_ref[j, :, ring * block * columns : ring * block * (columns + 1)] = final[sides * j + columns] * scale[j, :, :1]

    arrived(packed.at[pl.ds(0, nb - 1)], send1)
    arrived(rows.at[pl.ds(0, (ring - 1 + (ny // sides * cores if sides > 1 else 0)) * block)], send2)
    pair(0).wait_send()
    if sides > 1:

        @pl.when(major)
        def _():
            pair(1).wait_send()
            pair(2).wait_send()
            arrived(mine.at[pl.ds(0, 3 * ny - 2)], send4)

        @pl.when(jnp.logical_not(major))
        def _():
            arrived(mine.at[pl.ds(0, ny - 1)], send4)

    else:
        arrived(mine.at[pl.ds(0, ny - 1)], send4)


def local(sizes, cycles, frames, cycle_map):
    sides, ny, cores, nb, maxp = sizes
    block, pixels = frames.shape
    ring = ny * cores
    ntm = sides * ring
    own = cycles // nb
    width, depth = own * maxp, nb * maxp // cores
    dma = pltpu.SemaphoreType.DMA
    return pl.pallas_call(
        functools.partial(kernel, sizes),
        out_shape=jax.ShapeDtypeStruct((own, block, ntm * block), jnp.float32),
        in_specs=[pl.BlockSpec(memory_space=pltpu.HBM)] * 2,
        out_specs=pl.BlockSpec(memory_space=pltpu.VMEM),
        scratch_shapes=[
            pltpu.VMEM((block, pixels), jnp.bfloat16),
            pltpu.VMEM((pixels // LANES, LANES), jnp.int32),
            pltpu.VMEM((nb, width), jnp.int32),
            pltpu.VMEM((nb, LANES), jnp.int32),
            pltpu.VMEM((nb, block, width), jnp.bfloat16),
            pltpu.VMEM((nb, block, width), jnp.bfloat16),
            pltpu.VMEM((own, cores, block, depth), jnp.bfloat16),
            pltpu.VMEM((own, block, LANES), jnp.float32),
            pltpu.VMEM((ntm * block, depth), jnp.bfloat16),
            pltpu.VMEM((3, ny, cores, block, ring * block), jnp.float32),
            pltpu.VMEM((3, ny, block, ring * block), jnp.float32),
            pltpu.VMEM((3 * ny, block, ring * block), jnp.float32),
            pltpu.VMEM((ny * sides, block, ring * block), jnp.float32),
            dma((2,)), dma, dma((3,)), dma, dma((2,)), dma((3,)), dma((3,)), dma, dma,
        ],
        compiler_params=pltpu.CompilerParams(
            collective_id=0, has_side_effects=True, vmem_limit_bytes=VMEM_LIMIT
        ),
    )(frames, cycle_map.reshape(pixels // LANES, LANES))


def solution(mesh):
    return jax.shard_map(
        functools.partial(local, (SIDES, ROWS_Y, CORES, mesh.shape["band"], MAXP), CYCLES),
        mesh=mesh,
        in_specs=(P("tm", "band"), P("band")),
        out_specs=P("band", "tm", None),
        check_vma=False,
    )
```

```python
import functools

import jax
import jax.numpy as jnp
from jax import lax
from jax.experimental import pallas as pl
from jax.experimental.pallas import tpu as pltpu
from jax.sharding import PartitionSpec as P

MESH = pl.DeviceIdType.MESH
CYCLES = 64
MAXP = 96
LANES = 128
SIDES, ROWS_Y, CORES = 2, 4, 2
HALVES = 2
EARLY = 8
VMEM_LIMIT = 107 * 512 * 1024


def kernel(
    sizes, frames_hbm, map_ref, out_ref,
    frames_ref, source_ref, shift_ref,
    packed, got, normed, scale, rows, blocks, theirs, mine, final,
    load_sem, send1, recv1, send2, recv2, send3, recv3, send4, recv4,
):
    sides, ny, cores, nb, maxp = sizes
    block, pixels = frames_ref.shape
    own = out_ref.shape[0]
    width = own * maxp
    depth = rows.shape[1]
    ring = ny * cores
    sub = block // HALVES
    window = width + LANES
    ntile = pixels // LANES
    need = window // LANES
    tm = lax.axis_index("tm")
    band = lax.axis_index("band")
    side, place, core = lax.div(tm, ring), lax.rem(tm, ring), lax.rem(tm, cores)
    y = lax.div(place, cores)
    far = sides - 1 - side
    major = lax.rem(y, sides) == side

    turns = ([2, 3, 1, 0] if ny == 4 else list(range(ny - 1, -1, -1)))
    lead = (own + 1) // 2
    split = min(-(-lead * maxp // LANES) * LANES, width)
    parts = [(0, 0, width), (1, 0, split)] + ([(1, split, width)] if split < width else [])

    def at_turn(i):
        return lax.rem(y + turns[i], ny)

    load_frames = pltpu.make_async_copy(frames_hbm, frames_ref, load_sem)
    load_frames.start()

    barrier = pltpu.get_barrier_semaphore()

    def loop(low, high, body):
        for k in range(low, high):
            body(k)

    def after(k):
        return lax.rem(band + k, nb)

    def beyond(k):
        return lax.rem(y + [0, ny // 2, 1, ny - 1][k], ny)

    def arrived(ref, sem):
        pltpu.make_async_copy(ref, ref, sem).wait()

    def greet(to_tm, to_band):
        pl.semaphore_signal(barrier, inc=1, device_id=(to_tm, to_band), device_id_type=MESH)

    loop(1, nb, lambda k: greet(tm, after(k)))
    loop(1, sides * ring, lambda k: greet(lax.rem(tm + k, sides * ring), band))

    first = own * lax.broadcasted_iota(jnp.int32, (nb, LANES), 0)

    def pixels_below(cycle):
        below = jnp.zeros((nb, LANES), jnp.int32)
        for t in range(ntile):
            below += jnp.where(map_ref[t : t + 1, :] < first + cycle, 1, 0)
        return jnp.sum(below.astype(jnp.float32), axis=1, keepdims=True).astype(jnp.int32)

    starts = [pixels_below(j) for j in range(own + 1)]
    tile = jnp.minimum(starts[0] // LANES, ntile - need)
    lane = lax.broadcasted_iota(jnp.int32, (nb, width), 1)
    source = jnp.full((nb, width), -1, jnp.int32)
    for j in range(own):
        slot = lane - maxp * j
        start, end = starts[0], starts[1]
        for cycle in range(1, own):
            here = at_turn(j) == cycle
            start = jnp.where(here, starts[cycle], start)
            end = jnp.where(here, starts[cycle + 1], end)
        inside = (slot >= 0) & (slot < end - start)
        source = jnp.where(inside, slot + (start - LANES * tile), source)
    source_ref[...] = source
    shift_ref[...] = jnp.broadcast_to(tile, (nb, LANES))
    load_frames.wait()

    pixel = lax.broadcasted_iota(jnp.int32, (window, width), 0)

    def pack(owner):
        shift = jnp.broadcast_to(shift_ref[pl.ds(owner, 1), :], (block, LANES))
        tiles = [frames_ref[:, LANES * t : LANES * (t + 1)] for t in range(ntile)]
        for level in reversed(range((ntile - need).bit_length())):
            step = 1 << level
            moved = ((shift & step) > 0).astype(jnp.float32).astype(jnp.bfloat16) > 0
            tiles = [
                jnp.where(moved, tiles[t + step], tiles[t]) if t + step < len(tiles) else tiles[t]
                for t in range(min(len(tiles), step - 1 + need))
            ]
        view = jnp.concatenate(tiles[:need], axis=1)
        onehot = jnp.where(pixel == source_ref[pl.ds(owner, 1), :], 1.0, 0.0).astype(jnp.bfloat16)
        return jnp.dot(view, onehot, preferred_element_type=jnp.float32).astype(jnp.bfloat16)

    def chunk(part, owner):
        half, low, high = parts[part]
        lines = pl.ds(half * sub, sub)
        return pltpu.make_async_remote_copy(
            src_ref=packed.at[owner, lines, pl.ds(low, high - low)], dst_ref=got.at[band, lines, pl.ds(low, high - low)],
            send_sem=send1, recv_sem=recv1.at[part], device_id=(tm, owner), device_id_type=MESH,
        )

    def piece(half, to_side, to, slot):
        return pltpu.make_async_remote_copy(
            src_ref=normed.at[to // cores, to % cores, pl.ds(half * sub, sub)],
            dst_ref=rows.at[pl.ds(pl.multiple_of(slot * block + half * sub, sub), sub)],
            send_sem=send2, recv_sem=recv2.at[0 if to_side is side else 1],
            device_id=(to_side * ring + to, band), device_id_type=MESH,
        )

    def spread(half, slots):
        lines = slice(half * sub, (half + 1) * sub)
        for i in slots:
            wide = jnp.concatenate(
                [got[b, lines, maxp * i : maxp * (i + 1)].astype(jnp.float32) for b in range(nb)], axis=1
            )
            total = jnp.sum(wide, axis=1, keepdims=True)
            count = jnp.sum((wide > 0).astype(jnp.float32), axis=1, keepdims=True)
            scale[at_turn(i), lines] = jnp.broadcast_to(1.0 / count, (sub, LANES))
            normal = (wide * (count / total)).astype(jnp.bfloat16)
            for k in range(cores):
                normed[at_turn(i), k, lines] = normal[:, depth * k : depth * (k + 1)]
        for i in slots:
            to = at_turn(i) * cores
            if sides > 1:

                @pl.when(lax.rem(at_turn(i), sides) == far)
                def _():
                    for k in range(cores):
                        piece(half, far, to + k, tm).start()

            if turns[i]:
                for k in range(cores):
                    piece(half, side, to + k, tm).start()
            else:
                piece(half, side, to + 1 - core, tm).start()
                rows[pl.ds(pl.multiple_of(tm * block + half * sub, sub), sub), :] = normed[y, core, lines]

    def prepare(k, carry):
        packed[after(k)] = pack(after(k))
        return carry

    def send_first(k, carry):
        chunk(0, after(k)).start()
        return carry

    def prepare_and_send(k, carry):
        prepare(k, carry)
        return send_first(k, carry)

    early = min(EARLY, nb - 1)
    lax.fori_loop(1, early + 1, prepare, 0)
    pl.semaphore_wait(barrier, nb + sides * ring - 2)
    lax.fori_loop(1, early + 1, send_first, 0)
    lax.fori_loop(early + 1, nb, prepare_and_send, 0)
    got[band] = pack(band)
    for part in range(1, len(parts)):
        loop(1, nb, lambda k: chunk(part, after(k)).start())
    for part, (half, low, high) in enumerate(parts):
        arrived(got.at[pl.ds(0, nb - 1), pl.ds(0, sub), pl.ds(low, high - low)], recv1.at[part])
        if part == 0:
            spread(0, range(own))
        elif part == 1:
            spread(1, range(lead))
    spread(1, range(lead, own))

    def gram(kind):
        side_of = lambda other: pl.ds(pl.multiple_of((far if other else side) * ring * block, ring * block), ring * block)
        blocks[kind] = lax.dot_general(
            rows[side_of(kind == 2), :], rows[side_of(kind == 1), :], (((1,), (1,)), ((), ())),
            preferred_element_type=jnp.float32,
        ).reshape(blocks.shape[1:])
        pair(kind).start()

    def pair(kind):
        return pltpu.make_async_remote_copy(
            src_ref=blocks.at[kind, pl.ds(0, ny), 1 - core], dst_ref=theirs.at[kind],
            send_sem=send3.at[kind], recv_sem=recv3.at[kind],
            device_id=(side * ring + y * cores + 1 - core, band), device_id_type=MESH,
        )

    def result(kind, i, slot, columns):
        return pltpu.make_async_remote_copy(
            src_ref=mine.at[kind * ny + i], dst_ref=final.at[slot * sides + columns], send_sem=send4, recv_sem=recv4,
            device_id=((far if kind == 2 else side) * ring + i * cores + core, band), device_id_type=MESH,
        )

    def finish(kind):
        pair(kind).wait_recv()
        mine[ny * kind : ny * (kind + 1)] = blocks[kind, :, core] + theirs[kind]
        if kind == 2:
            loop(0, ny, lambda k: result(2, beyond((k + 1) % ny), y, side).start())
        else:
            columns = side if kind == 0 else far
            loop(1, ny, lambda k: result(kind, beyond(k), y, columns).start())
            final[y * sides + columns] = mine[ny * kind + y]

    arrived(rows.at[pl.ds(0, (ring - 1) * block)], recv2.at[0])
    gram(0)
    if sides > 1:

        @pl.when(major)
        def _():
            arrived(rows.at[pl.ds(0, ring * block)], recv2.at[1])
            gram(2)
            gram(1)
            finish(2)
            finish(1)

    finish(0)

    if sides > 1:

        @pl.when(major)
        def _():
            arrived(final.at[pl.ds(0, (ny - 1) * sides)], recv4)

        @pl.when(jnp.logical_not(major))
        def _():
            arrived(final.at[pl.ds(0, ny * sides - 1)], recv4)

    else:
        arrived(final.at[pl.ds(0, ny - 1)], recv4)

    for j in range(own):
        for columns in range(sides):
            out_ref[j, :, ring * block * columns : ring * block * (columns + 1)] = final[sides * j + columns] * scale[j, :, :1]

    arrived(packed.at[pl.ds(0, nb - 1)], send1)
    arrived(rows.at[pl.ds(0, (ring - 1 + (ny // sides * cores if sides > 1 else 0)) * block)], send2)
    pair(0).wait_send()
    if sides > 1:

        @pl.when(major)
        def _():
            pair(1).wait_send()
            pair(2).wait_send()
            arrived(mine.at[pl.ds(0, 3 * ny - 2)], send4)

        @pl.when(jnp.logical_not(major))
        def _():
            arrived(mine.at[pl.ds(0, ny - 1)], send4)

    else:
        arrived(mine.at[pl.ds(0, ny - 1)], send4)


def local(sizes, cycles, frames, cycle_map):
    sides, ny, cores, nb, maxp = sizes
    block, pixels = frames.shape
    ring = ny * cores
    ntm = sides * ring
    own = cycles // nb
    width, depth = own * maxp, nb * maxp // cores
    dma = pltpu.SemaphoreType.DMA
    return pl.pallas_call(
        functools.partial(kernel, sizes),
        out_shape=jax.ShapeDtypeStruct((own, block, ntm * block), jnp.float32),
        in_specs=[pl.BlockSpec(memory_space=pltpu.HBM), pl.BlockSpec(memory_space=pltpu.VMEM)],
        out_specs=pl.BlockSpec(memory_space=pltpu.VMEM),
        scratch_shapes=[
            pltpu.VMEM((block, pixels), jnp.bfloat16),
            pltpu.VMEM((nb, width), jnp.int32),
            pltpu.VMEM((nb, LANES), jnp.int32),
            pltpu.VMEM((nb, block, width), jnp.bfloat16),
            pltpu.VMEM((nb, block, width), jnp.bfloat16),
            pltpu.VMEM((own, cores, block, depth), jnp.bfloat16),
            pltpu.VMEM((own, block, LANES), jnp.float32),
            pltpu.VMEM((ntm * block, depth), jnp.bfloat16),
            pltpu.VMEM((3, ny, cores, block, ring * block), jnp.float32),
            pltpu.VMEM((3, ny, block, ring * block), jnp.float32),
            pltpu.VMEM((3 * ny, block, ring * block), jnp.float32),
            pltpu.VMEM((ny * sides, block, ring * block), jnp.float32),
            dma, dma, dma((3,)), dma, dma((2,)), dma((3,)), dma((3,)), dma, dma,
        ],
        compiler_params=pltpu.CompilerParams(
            collective_id=0, has_side_effects=True, vmem_limit_bytes=VMEM_LIMIT
        ),
    )(frames, cycle_map.reshape(pixels // LANES, LANES))


def solution(mesh):
    return jax.shard_map(
        functools.partial(local, (SIDES, ROWS_Y, CORES, mesh.shape["band"], MAXP), CYCLES),
        mesh=mesh,
        in_specs=(P("tm", "band"), P("band")),
        out_specs=P("band", "tm", None),
        check_vma=False,
    )
```

```python
import functools

import jax
import jax.numpy as jnp
from jax import lax
from jax.experimental import pallas as pl
from jax.experimental.pallas import tpu as pltpu
from jax.sharding import PartitionSpec as P

MESH = pl.DeviceIdType.MESH
CYCLES = 64
MAXP = 96
LANES = 128
SIDES, ROWS_Y, CORES = 2, 4, 2
HALVES = 2
EARLY = 8
VMEM_LIMIT = 107 * 512 * 1024


def kernel(
    sizes, frames_hbm, map_ref, out_ref,
    frames_ref, source_ref, shift_ref,
    packed, got, normed, scale, rows, blocks, theirs, mine, final,
    load_sem, send1, recv1, send2, recv2, send3, recv3, send4, recv4,
):
    sides, ny, cores, nb, maxp = sizes
    block, pixels = frames_ref.shape
    own = out_ref.shape[0]
    width = own * maxp
    depth = rows.shape[1]
    ring = ny * cores
    sub = block // HALVES
    window = width + LANES
    ntile = pixels // LANES
    need = window // LANES
    tm = lax.axis_index("tm")
    band = lax.axis_index("band")
    side, place, core = lax.div(tm, ring), lax.rem(tm, ring), lax.rem(tm, cores)
    y = lax.div(place, cores)
    far = sides - 1 - side
    major = lax.rem(y, sides) == side

    turns = ([2, 3, 1, 0] if ny == 4 else list(range(ny - 1, -1, -1)))
    lead = (own + 1) // 2
    split = min(-(-lead * maxp // LANES) * LANES, width)
    parts = [(0, 0, width), (1, 0, split)] + ([(1, split, width)] if split < width else [])

    def at_turn(i):
        return lax.rem(y + turns[i], ny)

    load_frames = pltpu.make_async_copy(frames_hbm, frames_ref, load_sem)
    load_frames.start()

    barrier = pltpu.get_barrier_semaphore()

    def loop(low, high, body):
        for k in range(low, high):
            body(k)

    def after(k):
        return lax.rem(band + k, nb)

    def beyond(k):
        return lax.rem(y + [0, ny // 2, 1, ny - 1][k], ny)

    def arrived(ref, sem):
        pltpu.make_async_copy(ref, ref, sem).wait()

    def greet(to_tm, to_band):
        pl.semaphore_signal(barrier, inc=1, device_id=(to_tm, to_band), device_id_type=MESH)

    loop(1, nb, lambda k: greet(tm, after(k)))
    loop(1, sides * ring, lambda k: greet(lax.rem(tm + k, sides * ring), band))

    first = own * lax.broadcasted_iota(jnp.int32, (nb, LANES), 0)

    def pixels_below(cycle):
        below = jnp.zeros((nb, LANES), jnp.int32)
        for t in range(ntile):
            below += jnp.where(map_ref[t : t + 1, :] < first + cycle, 1, 0)
        return jnp.sum(below.astype(jnp.float32), axis=1, keepdims=True).astype(jnp.int32)

    starts = [pixels_below(j) for j in range(own + 1)]
    tile = jnp.minimum(starts[0] // LANES, ntile - need)
    lane = lax.broadcasted_iota(jnp.int32, (nb, width), 1)
    source = jnp.full((nb, width), -1, jnp.int32)
    for j in range(own):
        slot = lane - maxp * j
        start, end = starts[0], starts[1]
        for cycle in range(1, own):
            here = at_turn(j) == cycle
            start = jnp.where(here, starts[cycle], start)
            end = jnp.where(here, starts[cycle + 1], end)
        inside = (slot >= 0) & (slot < end - start)
        source = jnp.where(inside, slot + (start - LANES * tile), source)
    source_ref[...] = source
    shift_ref[...] = jnp.broadcast_to(tile, (nb, LANES))
    load_frames.wait()

    pixel = lax.broadcasted_iota(jnp.int32, (window, width), 0)

    def pack(owner):
        shift = jnp.broadcast_to(shift_ref[pl.ds(owner, 1), :], (block, LANES))
        tiles = [frames_ref[:, LANES * t : LANES * (t + 1)] for t in range(ntile)]
        for level in reversed(range((ntile - need).bit_length())):
            step = 1 << level
            moved = ((shift & step) > 0).astype(jnp.float32).astype(jnp.bfloat16) > 0
            tiles = [
                jnp.where(moved, tiles[t + step], tiles[t]) if t + step < len(tiles) else tiles[t]
                for t in range(min(len(tiles), step - 1 + need))
            ]
        view = jnp.concatenate(tiles[:need], axis=1)
        onehot = jnp.where(pixel == source_ref[pl.ds(owner, 1), :], 1.0, 0.0).astype(jnp.bfloat16)
        return jnp.dot(view, onehot, preferred_element_type=jnp.float32).astype(jnp.bfloat16)

    def chunk(part, owner):
        half, low, high = parts[part]
        lines = pl.ds(half * sub, sub)
        return pltpu.make_async_remote_copy(
            src_ref=packed.at[owner, lines, pl.ds(low, high - low)], dst_ref=got.at[band, lines, pl.ds(low, high - low)],
            send_sem=send1, recv_sem=recv1.at[part], device_id=(tm, owner), device_id_type=MESH,
        )

    def piece(half, to_side, to, slot):
        return pltpu.make_async_remote_copy(
            src_ref=normed.at[to // cores, to % cores, pl.ds(half * sub, sub)],
            dst_ref=rows.at[pl.ds(pl.multiple_of(slot * block + half * sub, sub), sub)],
            send_sem=send2, recv_sem=recv2.at[0 if to_side is side else 1],
            device_id=(to_side * ring + to, band), device_id_type=MESH,
        )

    def spread(half, slots):
        lines = slice(half * sub, (half + 1) * sub)
        for i in slots:
            wide = jnp.concatenate(
                [got[b, lines, maxp * i : maxp * (i + 1)].astype(jnp.float32) for b in range(nb)], axis=1
            )
            total = jnp.sum(wide, axis=1, keepdims=True)
            count = jnp.sum((wide > 0).astype(jnp.float32), axis=1, keepdims=True)
            scale[at_turn(i), lines] = jnp.broadcast_to(1.0 / count, (sub, LANES))
            normal = (wide * (count / total)).astype(jnp.bfloat16)
            for k in range(cores):
                normed[at_turn(i), k, lines] = normal[:, depth * k : depth * (k + 1)]
        for i in slots:
            to = at_turn(i) * cores
            if sides > 1:

                @pl.when(lax.rem(at_turn(i), sides) == far)
                def _():
                    for k in range(cores):
                        piece(half, far, to + k, tm).start()

            if turns[i]:
                for k in range(cores):
                    piece(half, side, to + k, tm).start()
            else:
                piece(half, side, to + 1 - core, tm).start()
                rows[pl.ds(pl.multiple_of(tm * block + half * sub, sub), sub), :] = normed[y, core, lines]

    def prepare(k, carry):
        packed[after(k)] = pack(after(k))
        return carry

    def send_first(k, carry):
        chunk(0, after(k)).start()
        return carry

    def prepare_and_send(k, carry):
        prepare(k, carry)
        return send_first(k, carry)

    early = min(EARLY, nb - 1)
    lax.fori_loop(1, early + 1, prepare, 0)
    pl.semaphore_wait(barrier, nb + sides * ring - 2)
    lax.fori_loop(1, early + 1, send_first, 0)
    lax.fori_loop(early + 1, nb, prepare_and_send, 0)
    for part in range(1, len(parts)):
        loop(1, nb, lambda k: chunk(part, after(k)).start())
    got[band] = pack(band)
    for part, (half, low, high) in enumerate(parts):
        arrived(got.at[pl.ds(0, nb - 1), pl.ds(0, sub), pl.ds(low, high - low)], recv1.at[part])
        if part == 0:
            spread(0, range(own))
        elif part == 1:
            spread(1, range(lead))
    spread(1, range(lead, own))

    def gram(kind):
        side_of = lambda other: pl.ds(pl.multiple_of((far if other else side) * ring * block, ring * block), ring * block)
        blocks[kind] = lax.dot_general(
            rows[side_of(kind == 2), :], rows[side_of(kind == 1), :], (((1,), (1,)), ((), ())),
            preferred_element_type=jnp.float32,
        ).reshape(blocks.shape[1:])
        pair(kind).start()

    def pair(kind):
        return pltpu.make_async_remote_copy(
            src_ref=blocks.at[kind, pl.ds(0, ny), 1 - core], dst_ref=theirs.at[kind],
            send_sem=send3.at[kind], recv_sem=recv3.at[kind],
            device_id=(side * ring + y * cores + 1 - core, band), device_id_type=MESH,
        )

    def result(kind, i, slot, columns):
        return pltpu.make_async_remote_copy(
            src_ref=mine.at[kind * ny + i], dst_ref=final.at[slot * sides + columns], send_sem=send4, recv_sem=recv4,
            device_id=((far if kind == 2 else side) * ring + i * cores + core, band), device_id_type=MESH,
        )

    def finish(kind):
        pair(kind).wait_recv()
        mine[ny * kind : ny * (kind + 1)] = blocks[kind, :, core] + theirs[kind]
        if kind == 2:
            loop(0, ny, lambda k: result(2, beyond((k + 1) % ny), y, side).start())
        else:
            columns = side if kind == 0 else far
            loop(1, ny, lambda k: result(kind, beyond(k), y, columns).start())
            final[y * sides + columns] = mine[ny * kind + y]

    arrived(rows.at[pl.ds(0, (ring - 1) * block)], recv2.at[0])
    gram(0)
    if sides > 1:

        @pl.when(major)
        def _():
            arrived(rows.at[pl.ds(0, ring * block)], recv2.at[1])
            gram(2)
            gram(1)
            finish(2)
            finish(1)

    finish(0)

    if sides > 1:

        @pl.when(major)
        def _():
            arrived(final.at[pl.ds(0, (ny - 1) * sides)], recv4)

        @pl.when(jnp.logical_not(major))
        def _():
            arrived(final.at[pl.ds(0, ny * sides - 1)], recv4)

    else:
        arrived(final.at[pl.ds(0, ny - 1)], recv4)

    for j in range(own):
        for columns in range(sides):
            out_ref[j, :, ring * block * columns : ring * block * (columns + 1)] = final[sides * j + columns] * scale[j, :, :1]

    arrived(packed.at[pl.ds(0, nb - 1)], send1)
    arrived(rows.at[pl.ds(0, (ring - 1 + (ny // sides * cores if sides > 1 else 0)) * block)], send2)
    pair(0).wait_send()
    if sides > 1:

        @pl.when(major)
        def _():
            pair(1).wait_send()
            pair(2).wait_send()
            arrived(mine.at[pl.ds(0, 3 * ny - 2)], send4)

        @pl.when(jnp.logical_not(major))
        def _():
            arrived(mine.at[pl.ds(0, ny - 1)], send4)

    else:
        arrived(mine.at[pl.ds(0, ny - 1)], send4)


def local(sizes, cycles, frames, cycle_map):
    sides, ny, cores, nb, maxp = sizes
    block, pixels = frames.shape
    ring = ny * cores
    ntm = sides * ring
    own = cycles // nb
    width, depth = own * maxp, nb * maxp // cores
    dma = pltpu.SemaphoreType.DMA
    return pl.pallas_call(
        functools.partial(kernel, sizes),
        out_shape=jax.ShapeDtypeStruct((own, block, ntm * block), jnp.float32),
        in_specs=[pl.BlockSpec(memory_space=pltpu.HBM), pl.BlockSpec(memory_space=pltpu.VMEM)],
        out_specs=pl.BlockSpec(memory_space=pltpu.VMEM),
        scratch_shapes=[
            pltpu.VMEM((block, pixels), jnp.bfloat16),
            pltpu.VMEM((nb, width), jnp.int32),
            pltpu.VMEM((nb, LANES), jnp.int32),
            pltpu.VMEM((nb, block, width), jnp.bfloat16),
            pltpu.VMEM((nb, block, width), jnp.bfloat16),
            pltpu.VMEM((own, cores, block, depth), jnp.bfloat16),
            pltpu.VMEM((own, block, LANES), jnp.float32),
            pltpu.VMEM((ntm * block, depth), jnp.bfloat16),
            pltpu.VMEM((3, ny, cores, block, ring * block), jnp.float32),
            pltpu.VMEM((3, ny, block, ring * block), jnp.float32),
            pltpu.VMEM((3 * ny, block, ring * block), jnp.float32),
            pltpu.VMEM((ny * sides, block, ring * block), jnp.float32),
            dma, dma, dma((3,)), dma, dma((2,)), dma((3,)), dma((3,)), dma, dma,
        ],
        compiler_params=pltpu.CompilerParams(
            collective_id=0, has_side_effects=True, vmem_limit_bytes=VMEM_LIMIT
        ),
    )(frames, cycle_map.reshape(pixels // LANES, LANES))


def solution(mesh):
    return jax.shard_map(
        functools.partial(local, (SIDES, ROWS_Y, CORES, mesh.shape["band"], MAXP), CYCLES),
        mesh=mesh,
        in_specs=(P("tm", "band"), P("band")),
        out_specs=P("band", "tm", None),
        check_vma=False,
    )
```

```python
import functools

import jax
import jax.numpy as jnp
from jax import lax
from jax.experimental import pallas as pl
from jax.experimental.pallas import tpu as pltpu
from jax.sharding import PartitionSpec as P

MESH = pl.DeviceIdType.MESH
CYCLES = 64
MAXP = 96
LANES = 128
SIDES, ROWS_Y, CORES = 2, 4, 2
HALVES = 2
EARLY = 8
VMEM_LIMIT = 107 * 512 * 1024


def kernel(
    sizes, frames_hbm, map_ref, out_ref,
    frames_ref, source_ref, shift_ref,
    packed, got, normed, scale, rows, blocks, theirs, mine, final,
    load_sem, send1, recv1, send2, recv2, send3, recv3, send4, recv4,
):
    sides, ny, cores, nb, maxp = sizes
    block, pixels = frames_ref.shape
    own = out_ref.shape[0]
    width = own * maxp
    depth = rows.shape[1]
    ring = ny * cores
    sub = block // HALVES
    window = width + LANES
    ntile = pixels // LANES
    need = window // LANES
    tm = lax.axis_index("tm")
    band = lax.axis_index("band")
    side, place, core = lax.div(tm, ring), lax.rem(tm, ring), lax.rem(tm, cores)
    y = lax.div(place, cores)
    far = sides - 1 - side
    major = lax.rem(y, sides) == side

    turns = ([2, 3, 1, 0] if ny == 4 else list(range(ny - 1, -1, -1)))
    lead = (own + 1) // 2
    split = min(-(-lead * maxp // LANES) * LANES, width)
    parts = [(0, 0, width), (1, 0, split)] + ([(1, split, width)] if split < width else [])

    def at_turn(i):
        return lax.rem(y + turns[i], ny)

    load_frames = pltpu.make_async_copy(frames_hbm, frames_ref, load_sem)
    load_frames.start()

    barrier = pltpu.get_barrier_semaphore()

    def loop(low, high, body):
        for k in range(low, high):
            body(k)

    def after(k):
        return lax.rem(band + k, nb)

    def beyond(k):
        return lax.rem(y + [0, ny // 2, 1, ny - 1][k], ny)

    def arrived(ref, sem):
        pltpu.make_async_copy(ref, ref, sem).wait()

    def greet(to_tm, to_band):
        pl.semaphore_signal(barrier, inc=1, device_id=(to_tm, to_band), device_id_type=MESH)

    loop(1, nb, lambda k: greet(tm, after(k)))
    loop(1, sides * ring, lambda k: greet(lax.rem(tm + k, sides * ring), band))

    first = own * lax.broadcasted_iota(jnp.int32, (nb, LANES), 0)

    def pixels_below(cycle):
        below = jnp.zeros((nb, LANES), jnp.int32)
        for t in range(ntile):
            below += jnp.where(map_ref[t : t + 1, :] < first + cycle, 1, 0)
        return jnp.sum(below.astype(jnp.float32), axis=1, keepdims=True).astype(jnp.int32)

    starts = [pixels_below(j) for j in range(own + 1)]
    tile = jnp.minimum(starts[0] // LANES, ntile - need)
    lane = lax.broadcasted_iota(jnp.int32, (nb, width), 1)
    source = jnp.full((nb, width), -1, jnp.int32)
    for j in range(own):
        slot = lane - maxp * j
        start, end = starts[0], starts[1]
        for cycle in range(1, own):
            here = at_turn(j) == cycle
            start = jnp.where(here, starts[cycle], start)
            end = jnp.where(here, starts[cycle + 1], end)
        inside = (slot >= 0) & (slot < end - start)
        source = jnp.where(inside, slot + (start - LANES * tile), source)
    source_ref[...] = source
    shift_ref[...] = jnp.broadcast_to(tile, (nb, LANES))
    load_frames.wait()

    pixel = lax.broadcasted_iota(jnp.int32, (window, width), 0)

    def pack(owner):
        shift = jnp.broadcast_to(shift_ref[pl.ds(owner, 1), :], (block, LANES))
        tiles = [frames_ref[:, LANES * t : LANES * (t + 1)] for t in range(ntile)]
        for level in reversed(range((ntile - need).bit_length())):
            step = 1 << level
            moved = ((shift & step) > 0).astype(jnp.float32).astype(jnp.bfloat16) > 0
            tiles = [
                jnp.where(moved, tiles[t + step], tiles[t]) if t + step < len(tiles) else tiles[t]
                for t in range(min(len(tiles), step - 1 + need))
            ]
        view = jnp.concatenate(tiles[:need], axis=1)
        onehot = jnp.where(pixel == source_ref[pl.ds(owner, 1), :], 1.0, 0.0).astype(jnp.bfloat16)
        return jnp.dot(view, onehot, preferred_element_type=jnp.float32).astype(jnp.bfloat16)

    def chunk(part, owner):
        half, low, high = parts[part]
        lines = pl.ds(half * sub, sub)
        return pltpu.make_async_remote_copy(
            src_ref=packed.at[owner, lines, pl.ds(low, high - low)], dst_ref=got.at[band, lines, pl.ds(low, high - low)],
            send_sem=send1, recv_sem=recv1.at[part], device_id=(tm, owner), device_id_type=MESH,
        )

    def piece(half, to_side, to, slot):
        return pltpu.make_async_remote_copy(
            src_ref=normed.at[to // cores, to % cores, pl.ds(half * sub, sub)],
            dst_ref=rows.at[pl.ds(pl.multiple_of(slot * block + half * sub, sub), sub)],
            send_sem=send2, recv_sem=recv2.at[0 if to_side is side else 1],
            device_id=(to_side * ring + to, band), device_id_type=MESH,
        )

    def spread(half, slots):
        lines = slice(half * sub, (half + 1) * sub)
        for i in slots:
            wide = jnp.concatenate(
                [got[b, lines, maxp * i : maxp * (i + 1)].astype(jnp.float32) for b in range(nb)], axis=1
            )
            total = jnp.sum(wide, axis=1, keepdims=True)
            count = jnp.sum((wide > 0).astype(jnp.float32), axis=1, keepdims=True)
            scale[at_turn(i), lines] = jnp.broadcast_to(1.0 / count, (sub, LANES))
            normal = (wide * (count / total)).astype(jnp.bfloat16)
            for k in range(cores):
                normed[at_turn(i), k, lines] = normal[:, depth * k : depth * (k + 1)]
        for i in slots:
            to = at_turn(i) * cores
            if sides > 1:

                @pl.when(lax.rem(at_turn(i), sides) == far)
                def _():
                    for k in range(cores):
                        piece(half, far, to + k, tm).start()

            if turns[i]:
                for k in range(cores):
                    piece(half, side, to + k, tm).start()
            else:
                piece(half, side, to + 1 - core, tm).start()
                rows[pl.ds(pl.multiple_of(tm * block + half * sub, sub), sub), :] = normed[y, core, lines]

    def prepare(k, carry):
        packed[after(k)] = pack(after(k))
        return carry

    def send_first(k, carry):
        chunk(0, after(k)).start()
        return carry

    def prepare_and_send(k, carry):
        prepare(k, carry)
        return send_first(k, carry)

    early = min(EARLY, nb - 1)
    lax.fori_loop(1, early + 1, prepare, 0)
    pl.semaphore_wait(barrier, nb + sides * ring - 2)
    lax.fori_loop(1, early + 1, send_first, 0)
    lax.fori_loop(early + 1, nb, prepare_and_send, 0)
    got[band] = pack(band)
    for part in range(1, len(parts)):
        loop(1, nb, lambda k: chunk(part, after(k)).start())
    for part, (half, low, high) in enumerate(parts):
        arrived(got.at[pl.ds(0, nb - 1), pl.ds(0, sub), pl.ds(low, high - low)], recv1.at[part])
        if part == 0:
            spread(0, range(own))
        elif part == 1:
            spread(1, range(lead))
    spread(1, range(lead, own))

    def gram(kind):
        side_of = lambda other: pl.ds(pl.multiple_of((far if other else side) * ring * block, ring * block), ring * block)
        blocks[kind] = lax.dot_general(
            rows[side_of(kind == 2), :], rows[side_of(kind == 1), :], (((1,), (1,)), ((), ())),
            preferred_element_type=jnp.float32,
        ).reshape(blocks.shape[1:])
        pair(kind).start()

    def pair(kind):
        return pltpu.make_async_remote_copy(
            src_ref=blocks.at[kind, pl.ds(0, ny), 1 - core], dst_ref=theirs.at[kind],
            send_sem=send3.at[kind], recv_sem=recv3.at[kind],
            device_id=(side * ring + y * cores + 1 - core, band), device_id_type=MESH,
        )

    def result(kind, i, slot, columns):
        return pltpu.make_async_remote_copy(
            src_ref=mine.at[kind * ny + i], dst_ref=final.at[slot * sides + columns], send_sem=send4, recv_sem=recv4,
            device_id=((far if kind == 2 else side) * ring + i * cores + core, band), device_id_type=MESH,
        )

    def finish(kind):
        pair(kind).wait_recv()
        mine[ny * kind : ny * (kind + 1)] = blocks[kind, :, core] + theirs[kind]
        if kind == 2:
            loop(0, ny, lambda k: result(2, beyond((k + 1) % ny), y, side).start())
        else:
            columns = side if kind == 0 else far
            loop(1, ny, lambda k: result(kind, beyond(k), y, columns).start())
            final[y * sides + columns] = mine[ny * kind + y]

    arrived(rows.at[pl.ds(0, (ring - 1) * block)], recv2.at[0])
    gram(0)
    if sides > 1:

        @pl.when(major)
        def _():
            arrived(rows.at[pl.ds(0, ring * block)], recv2.at[1])
            gram(2)
            finish(0)
            gram(1)
            finish(2)
            finish(1)

        @pl.when(jnp.logical_not(major))
        def _():
            finish(0)

    else:
        finish(0)

    if sides > 1:

        @pl.when(major)
        def _():
            arrived(final.at[pl.ds(0, (ny - 1) * sides)], recv4)

        @pl.when(jnp.logical_not(major))
        def _():
            arrived(final.at[pl.ds(0, ny * sides - 1)], recv4)

    else:
        arrived(final.at[pl.ds(0, ny - 1)], recv4)

    for j in range(own):
        for columns in range(sides):
            out_ref[j, :, ring * block * columns : ring * block * (columns + 1)] = final[sides * j + columns] * scale[j, :, :1]

    arrived(packed.at[pl.ds(0, nb - 1)], send1)
    arrived(rows.at[pl.ds(0, (ring - 1 + (ny // sides * cores if sides > 1 else 0)) * block)], send2)
    pair(0).wait_send()
    if sides > 1:

        @pl.when(major)
        def _():
            pair(1).wait_send()
            pair(2).wait_send()
            arrived(mine.at[pl.ds(0, 3 * ny - 2)], send4)

        @pl.when(jnp.logical_not(major))
        def _():
            arrived(mine.at[pl.ds(0, ny - 1)], send4)

    else:
        arrived(mine.at[pl.ds(0, ny - 1)], send4)


def local(sizes, cycles, frames, cycle_map):
    sides, ny, cores, nb, maxp = sizes
    block, pixels = frames.shape
    ring = ny * cores
    ntm = sides * ring
    own = cycles // nb
    width, depth = own * maxp, nb * maxp // cores
    dma = pltpu.SemaphoreType.DMA
    return pl.pallas_call(
        functools.partial(kernel, sizes),
        out_shape=jax.ShapeDtypeStruct((own, block, ntm * block), jnp.float32),
        in_specs=[pl.BlockSpec(memory_space=pltpu.HBM), pl.BlockSpec(memory_space=pltpu.VMEM)],
        out_specs=pl.BlockSpec(memory_space=pltpu.VMEM),
        scratch_shapes=[
            pltpu.VMEM((block, pixels), jnp.bfloat16),
            pltpu.VMEM((nb, width), jnp.int32),
            pltpu.VMEM((nb, LANES), jnp.int32),
            pltpu.VMEM((nb, block, width), jnp.bfloat16),
            pltpu.VMEM((nb, block, width), jnp.bfloat16),
            pltpu.VMEM((own, cores, block, depth), jnp.bfloat16),
            pltpu.VMEM((own, block, LANES), jnp.float32),
            pltpu.VMEM((ntm * block, depth), jnp.bfloat16),
            pltpu.VMEM((3, ny, cores, block, ring * block), jnp.float32),
            pltpu.VMEM((3, ny, block, ring * block), jnp.float32),
            pltpu.VMEM((3 * ny, block, ring * block), jnp.float32),
            pltpu.VMEM((ny * sides, block, ring * block), jnp.float32),
            dma, dma, dma((3,)), dma, dma((2,)), dma((3,)), dma((3,)), dma, dma,
        ],
        compiler_params=pltpu.CompilerParams(
            collective_id=0, has_side_effects=True, vmem_limit_bytes=VMEM_LIMIT
        ),
    )(frames, cycle_map.reshape(pixels // LANES, LANES))


def solution(mesh):
    return jax.shard_map(
        functools.partial(local, (SIDES, ROWS_Y, CORES, mesh.shape["band"], MAXP), CYCLES),
        mesh=mesh,
        in_specs=(P("tm", "band"), P("band")),
        out_specs=P("band", "tm", None),
        check_vma=False,
    )
```
